256 devices in a mesh: rows: 32 (over y_lo, z, core), pairs: 8 (over x, y_hi).
Axes of the slice: x: 4, y: 4 (y_hi: 2, y_lo: 2; y = y_hi * 2 + y_lo), z: 8, core: 2. Of those that a mesh axis runs over, the one named last changes fastest.
Arguments:
- slab_active: float32 [64, 64, 4096], P('rows', None, 'pairs'), may hold values from -6 to 6
- slab_general: float32 [64, 1536, 4096], P('rows', None, 'pairs'), may hold values from -6 to 6
- kappa_general: float32 [1536, 64], P('rows'), may hold values from -0.15625 to 0.15625
- kappa_window: float32 [64, 64], P('rows'), as said below
- density_one: float32 [4096], P('pairs'), may hold values from -0.09375 to 0.09375
- density_two: bfloat16 [64, 64, 4096], P(None, None, 'pairs'), may hold values from -0.01171875 to 0.01171875
Outputs:
- sigma_vector: float32 [64, 64], P('rows')
The draws below stay inside these ranges and needn't reach their ends.
Inputs may be any that keep to these rules, and one draw needn't show every extreme that they name: kappa_window is antisymmetric: kappa_window[p, q] = -kappa_window[q, p] exactly, with zero diagonal.
All inputs are finite; a program needn't handle non-finite values.
Results may differ from the reference program's by a relative error of at most 0.0003.
Values sent between devices are 32-bit elements; how exact they have to be, the bound alone decides.
A program may use at most 64 MiB of HBM per device.

```python
import jax
import jax.numpy as jnp
from jax import lax

N = 1536
A = 64
PAIRS = 4096
NP = 64


def draw_kappa_window(key, part):
    key = jax.random.fold_in(key, 7)
    base = jax.random.normal(key, (NP, NP), jnp.float32)
    return (base - base.T) * (0.7 / NP ** 0.5)


def shard_levels(stream_key, dims, pieces, low, top_value):
    loudness = 1.0
    for position, shards_of in pieces:
        draws = jax.random.uniform(jax.random.fold_in(jax.random.fold_in(stream_key, 6), position), (shards_of,), jnp.float32, low / len(pieces), top_value / len(pieces))
        loudness = loudness * jnp.repeat(jnp.exp(draws), dims[position] // shards_of).reshape((-1,) + (1,) * (len(dims) - 1 - position))
    return loudness


def normal_values(rng, dims, scale, limit, pieces=(), dtype=jnp.bfloat16):
    result = scale * jax.random.normal(rng, dims, jnp.float32)
    if pieces:
        result = result * shard_levels(rng, dims, pieces, -0.22, 0.18)
    return jnp.clip(result, -limit, limit).astype(dtype)


def setup_inputs(seed: int = 0) -> dict:
    keys = jax.random.split(jax.random.key(seed), 7)
    return {
        "slab_active": normal_values(keys[0], (NP, A, PAIRS), 1.0, 6.0, ((0, 32), (2, 8)), jnp.float32),
        "slab_general": normal_values(keys[1], (NP, N, PAIRS), 1.0, 6.0, ((0, 32), (2, 8)), jnp.float32),
        "kappa_general": normal_values(keys[2], (N, A), N ** -0.5, 0.15625, ((0, 32),), jnp.float32),
        "kappa_window": draw_kappa_window(jax.random.fold_in(keys[6], 71), 0),
        "density_one": normal_values(keys[4], (PAIRS,), PAIRS ** -0.5, 0.09375, ((0, 8),), jnp.float32),
        "density_two": normal_values(keys[5], (A, A, PAIRS), (A * PAIRS) ** -0.5, 0.01171875, ((2, 8),)),
    }


def reference(slab_active, slab_general, kappa_general, kappa_window, density_one, density_two):
    highest = lax.Precision.HIGHEST
    moved = jnp.einsum("pqc,qt->ptc", slab_general, kappa_general, precision=highest)
    turned = jnp.einsum("pq,qtc->ptc", kappa_window, slab_active, precision=highest)
    total = moved + turned
    exchange_term = jnp.einsum("puc,tuc->pt", total, density_two.astype(jnp.float32), precision=highest)
    coulomb_term = jnp.einsum("ptc,c->pt", moved, density_one, precision=highest)
    return 2.0 * (exchange_term + 2.0 * coulomb_term)
```

```python
import jax
import jax.numpy as jnp
from jax import lax
from jax.experimental import pallas as pl
from jax.experimental.pallas import tpu as pltpu
from jax.sharding import PartitionSpec as P

MESH = pl.DeviceIdType.MESH
BF16, F32 = jnp.bfloat16, jnp.float32
ROW_BY_ROW = (((1,), (1,)), ((), ()))
PLAIN = (((1,), (0,)), ((), ()))

NEAR = ((0, 0), (0, 1), (0, 7), (1, 0), (0, 2), (0, 6), (1, 1), (1, 7))
FAR = ((0, 3), (0, 5), (1, 2), (1, 6), (0, 4), (1, 3), (1, 5), (1, 4))
PLACES = (NEAR, FAR)
SEND_ORDER = tuple(reversed(FAR)) + tuple(reversed(NEAR[1:]))


def slot_of(dy, dz):
    for chunk in range(2):
        if (dy, dz) in PLACES[chunk]:
            return chunk, PLACES[chunk].index((dy, dz))


def split(x):
    high = x.astype(BF16)
    return high, (x - high.astype(F32)).astype(BF16)


def cross(d2_ref, w_ref, s8_ref):
    sub = lax.broadcasted_iota(jnp.int32, (8, 256), 0)
    lane = lax.broadcasted_iota(jnp.int32, (8, 256), 1) % 64
    masks = [lane == sub + 8 * k for k in range(8)]
    group = 8
    for b in range(64 // group):
        r = lax.dot_general(
            d2_ref[b * group:(b + 1) * group].reshape(group * 64, 512), w_ref[...], ROW_BY_ROW,
            preferred_element_type=F32,
        )
        for t in range(group):
            acc = jnp.zeros((8, 256), F32)
            for k in range(8):
                at = (t * 8 + k) * 8
                acc = jnp.where(masks[k], r[at:at + 8, :], acc)
            s8_ref[b * group + t] = acc


def as_row(s8_ref):
    s = jnp.sum(s8_ref[...], axis=1).T
    pair = jnp.sum(s.reshape(2, 2, 64, 64), axis=(0, 2))
    return jnp.concatenate([pair[0:1], pair[1:2]], axis=1)


def kernel(
    sa_hbm, g_hbm, kg_hbm, kw_hbm, d1_hbm, d2_hbm, out_ref,
    sa, gbuf, kgin, kw, d1, d2, ghi, glo, kgbuf, left, w, s8, moved, fall, pbuf,
    load_sem, kg_send, kg_recv, f_send, f_recv, sib_send, sib_recv, p_send, p_recv,
):
    row, pair = lax.axis_index("rows"), lax.axis_index("pairs")
    core = row % 2
    chip = row // 2
    ylo, z = chip // 8, chip % 8

    def chip_at(dy, dz):
        return lax.rem(ylo + dy, 2) * 8 + lax.rem(z + dz, 8)

    def peer(dy, dz):
        return (chip_at(dy, dz) * 2 + core, pair)

    sibling = (chip * 2 + 1 - core, pair)
    pair_peers = [(row, lax.rem(pair + k, 8)) for k in range(1, 8)]

    kg_load = pltpu.make_async_copy(kg_hbm, kgin, load_sem.at[0])
    kg_load.start()
    barrier = pltpu.get_barrier_semaphore()
    for dy, dz in SEND_ORDER:
        pl.semaphore_signal(barrier, inc=1, device_id=peer(dy, dz), device_id_type=MESH)
    for dev in pair_peers + [sibling]:
        pl.semaphore_signal(barrier, inc=1, device_id=dev, device_id_type=MESH)
    sa_load = pltpu.make_async_copy(sa_hbm, sa, load_sem.at[1])
    sa_load.start()
    d2_load = pltpu.make_async_copy(d2_hbm, d2, load_sem.at[2])
    d2_load.start()
    d1_load = pltpu.make_async_copy(d1_hbm, d1, load_sem.at[3])
    d1_load.start()
    kw_load = pltpu.make_async_copy(kw_hbm, kw, load_sem.at[4])
    kw_load.start()
    g_loads = []
    for p in range(2):
        for h in range(2):
            load = pltpu.make_async_copy(
                g_hbm.at[p, :, pl.ds(h * 24, 24), :], gbuf.at[p, h], load_sem.at[5 + 2 * p + h]
            )
            load.start()
            g_loads.append(load)

    kg_load.wait()
    kgbuf[0, core, 0] = jnp.concatenate([kgin[0:24, :], kgin[24:48, :]], axis=1)
    pl.semaphore_wait(barrier, 23)

    kg_copies = {}
    for n, (dy, dz) in enumerate(SEND_ORDER):
        chunk, slot = slot_of(dy, (8 - dz) % 8)
        copy = pltpu.make_async_remote_copy(
            kgbuf.at[0, core, 0], kgbuf.at[chunk, core, slot], kg_send.at[n], kg_recv.at[chunk, slot],
            device_id=peer(dy, dz), device_id_type=MESH,
        )
        copy.start()
        kg_copies[chunk, slot] = copy

    sa_load.wait()
    high, low = split(sa[...].reshape(128, 512))
    w[0:128] = high
    w[128:256] = low
    d2_load.wait()
    cross(d2, w, s8)
    fall[core, chip] = as_row(s8)
    f_copies = []
    for n, (dy, dz) in enumerate(SEND_ORDER):
        copy = pltpu.make_async_remote_copy(
            fall.at[core, chip], fall.at[core, chip], f_send.at[n], f_recv.at[n],
            device_id=peer(dy, dz), device_id_type=MESH,
        )
        copy.start()
        f_copies.append(copy)

    for load in g_loads:
        load.wait()

    def split_general(n, _):
        p, h, c = n // 4, (n // 2) % 2, n % 2
        for chunk in range(2):
            for s in range(0, 8, 2):
                first, second = (chip_at(*PLACES[chunk][s + i]) * 2 + c for i in range(2))
                both = jnp.concatenate([gbuf[p, h, first], gbuf[p, h, second]], axis=0)
                a, b = split(both)
                ghi[chunk, p, h, c, s * 24:s * 24 + 48, :] = a
                glo[chunk, p, h, c, s * 24:s * 24 + 48, :] = b
        return 0

    lax.fori_loop(0, 8, split_general, 0)

    def hand_over(chunk):
        for slot in range(8):
            if (chunk, slot) != (0, 0):
                kg_copies[chunk, slot].wait_recv()
        copy = pltpu.make_async_remote_copy(
            kgbuf.at[chunk, core], kgbuf.at[chunk, core], sib_send.at[chunk], sib_recv.at[chunk],
            device_id=sibling, device_id_type=MESH,
        )
        copy.start()
        return copy

    def rotate(chunk):
        x = kgbuf[chunk].reshape(384, 128).T
        high, low = split(jnp.concatenate([x[0:64], x[64:128]], axis=1))
        left[0:64] = high
        left[64:128] = low
        for p in range(2):
            gh = ghi[chunk, p].reshape(768, 512)
            gl = glo[chunk, p].reshape(768, 512)
            a = lax.dot_general(left[...], gh, PLAIN, preferred_element_type=F32)
            b = lax.dot_general(left[0:64], gl, PLAIN, preferred_element_type=F32)
            part = a[0:64] + a[64:128] + b
            moved[p] = part if chunk == 0 else moved[p] + part

    near = hand_over(0)
    near.wait_recv()
    rotate(0)
    far = hand_over(1)

    for copy in f_copies:
        copy.wait_recv()
    f_over = pltpu.make_async_remote_copy(
        fall.at[core], fall.at[core], sib_send.at[2], sib_recv.at[2], device_id=sibling, device_id_type=MESH,
    )
    f_over.start()

    far.wait_recv()
    rotate(1)
    high, low = split(moved[...].reshape(128, 512))
    w[0:128] = high
    w[128:256] = low
    cross(d2, w, s8)
    exchange = as_row(s8)

    d1_load.wait()
    high, low = split(jnp.broadcast_to(d1[...], (16, 512)))
    at = lax.broadcasted_iota(jnp.int32, (16, 512), 0)
    ones = jnp.where(at == 0, high.astype(F32), jnp.where(at == 1, low.astype(F32), 0.0)).astype(BF16)
    c = lax.dot_general(ones, w[...], ROW_BY_ROW, preferred_element_type=F32)
    c = c[0:1] + c[1:2]
    coulomb = c[:, 0:128] + c[:, 128:256]

    kw_load.wait()
    f_over.wait_recv()
    lane = lax.broadcasted_iota(jnp.int32, (1, 128), 1)
    acc = [jnp.zeros((1, 128), F32) for _ in range(2)]
    for k in range(16):
        for c in range(2):
            f = fall[c, k]
            for p in range(2):
                q = 4 * k + 2 * c
                acc[p] = acc[p] + f * jnp.where(lane < 64, kw[p, q], kw[p, q + 1])
    turned = jnp.concatenate([a[:, 0:64] + a[:, 64:128] for a in acc], axis=1)

    pbuf[pair] = exchange + 2.0 * coulomb + turned
    p_copies = []
    for n, dev in enumerate(pair_peers):
        copy = pltpu.make_async_remote_copy(
            pbuf.at[pair], pbuf.at[pair], p_send.at[n], p_recv.at[n], device_id=dev, device_id_type=MESH,
        )
        copy.start()
        p_copies.append(copy)
    for copy in p_copies:
        copy.wait_recv()
    total = pbuf[0]
    for k in range(1, 8):
        total = total + pbuf[k]
    total = 2.0 * total
    out_ref[0:1, :] = total[:, 0:64]
    out_ref[1:2, :] = total[:, 64:128]

    for copy in list(kg_copies.values()) + f_copies + p_copies + [near, far, f_over]:
        copy.wait_send()


def per_device(slab_active, slab_general, kappa_general, kappa_window, density_one, density_two):
    dma = pltpu.SemaphoreType.DMA
    return pl.pallas_call(
        kernel,
        out_shape=jax.ShapeDtypeStruct((2, 64), F32),
        in_specs=[pl.BlockSpec(memory_space=pl.ANY)] * 6,
        out_specs=pl.BlockSpec(memory_space=pltpu.VMEM),
        scratch_shapes=[
            pltpu.VMEM((2, 64, 512), F32),
            pltpu.VMEM((2, 2, 32, 24, 512), F32),
            pltpu.VMEM((48, 64), F32),
            pltpu.SMEM((2, 64), F32),
            pltpu.VMEM((1, 512), F32),
            pltpu.VMEM((64, 64, 512), BF16),
            pltpu.VMEM((2, 2, 2, 2, 192, 512), BF16),
            pltpu.VMEM((2, 2, 2, 2, 192, 512), BF16),
            pltpu.VMEM((2, 2, 8, 24, 128), F32),
            pltpu.VMEM((128, 768), BF16),
            pltpu.VMEM((256, 512), BF16),
            pltpu.VMEM((64, 8, 256), F32),
            pltpu.VMEM((2, 64, 512), F32),
            pltpu.VMEM((2, 16, 1, 128), F32),
            pltpu.VMEM((8, 1, 128), F32),
            dma((9,)),
            dma((15,)),
            dma((2, 8)),
            dma((15,)),
            dma((15,)),
            dma((3,)),
            dma((3,)),
            dma((7,)),
            dma((7,)),
        ],
        compiler_params=pltpu.CompilerParams(
            collective_id=0, has_side_effects=True, vmem_limit_bytes=48 * 2**20
        ),
        name="sigma",
    )(
        slab_active,
        slab_general.reshape(2, 32, 48, 512),
        kappa_general,
        kappa_window,
        density_one.reshape(1, 512),
        density_two,
    )


def solution(mesh):
    in_specs = (
        P("rows", None, "pairs"),
        P("rows", None, "pairs"),
        P("rows", None),
        P("rows", None),
        P("pairs"),
        P(None, None, "pairs"),
    )
    out_specs = P("rows", None)
    return jax.shard_map(
        per_device, mesh=mesh, in_specs=in_specs, out_specs=out_specs, check_vma=False
    )
```

```python
import jax
import jax.numpy as jnp
from jax import lax
from jax.experimental import pallas as pl
from jax.experimental.pallas import tpu as pltpu
from jax.sharding import PartitionSpec as P

MESH = pl.DeviceIdType.MESH
BF16, F32 = jnp.bfloat16, jnp.float32
ROW_BY_ROW = (((1,), (1,)), ((), ()))
PLAIN = (((1,), (0,)), ((), ()))

NEAR = ((0, 0), (0, 1), (0, 7), (1, 0), (0, 2), (0, 6), (1, 1), (1, 7))
FAR = ((0, 3), (0, 5), (1, 2), (1, 6), (0, 4), (1, 3), (1, 5), (1, 4))
PLACES = (NEAR, FAR)
SEND_ORDER = tuple(reversed(FAR)) + tuple(reversed(NEAR[1:]))


def slot_of(dy, dz):
    for chunk in range(2):
        if (dy, dz) in PLACES[chunk]:
            return chunk, PLACES[chunk].index((dy, dz))


def split(x):
    high = x.astype(BF16)
    return high, (x - high.astype(F32)).astype(BF16)


def cross(d2_ref, w_ref, s8_ref):
    sub = lax.broadcasted_iota(jnp.int32, (8, 256), 0)
    lane = lax.broadcasted_iota(jnp.int32, (8, 256), 1) % 64
    masks = [lane == sub + 8 * k for k in range(8)]
    group = 8
    for b in range(64 // group):
        r = lax.dot_general(
            d2_ref[b * group:(b + 1) * group].reshape(group * 64, 512), w_ref[...], ROW_BY_ROW,
            preferred_element_type=F32,
        )
        for t in range(group):
            acc = jnp.zeros((8, 256), F32)
            for k in range(8):
                at = (t * 8 + k) * 8
                acc = jnp.where(masks[k], r[at:at + 8, :], acc)
            s8_ref[b * group + t] = acc


def as_row(s8_ref):
    s = jnp.sum(s8_ref[...], axis=1).T
    pair = jnp.sum(s.reshape(2, 2, 64, 64), axis=(0, 2))
    return jnp.concatenate([pair[0:1], pair[1:2]], axis=1)


def kernel(
    sa_hbm, g_hbm, kg_hbm, kw_hbm, d1_hbm, d2_hbm, out_ref,
    sa, gbuf, kgin, kw, d1, d2, ghi, glo, kgbuf, left, w, s8, moved, fall, pbuf,
    load_sem, here, kg_send, kg_recv, f_send, f_recv, sib_send, sib_recv, p_send, p_recv,
):
    row, pair = lax.axis_index("rows"), lax.axis_index("pairs")
    core = row % 2
    chip = row // 2
    ylo, z = chip // 8, chip % 8

    def chip_at(dy, dz):
        return lax.rem(ylo + dy, 2) * 8 + lax.rem(z + dz, 8)

    def peer(dy, dz):
        return (chip_at(dy, dz) * 2 + core, pair)

    def is_later(dy, dz):
        return lax.rem(z + dz, 8) * 2 + lax.rem(ylo + dy, 2) > z * 2 + ylo

    def number(dy, dz):
        return SEND_ORDER.index((dy, dz))

    sibling = (chip * 2 + 1 - core, pair)
    pair_peers = [lax.rem(pair + k, 8) for k in range(1, 8)]

    kg_load = pltpu.make_async_copy(kg_hbm, kgin, load_sem.at[0])
    kg_load.start()
    barrier = pltpu.get_barrier_semaphore()
    earlier = core
    for dy, dz in SEND_ORDER:
        later = is_later(dy, dz)
        earlier = earlier + jnp.where(later, 0, 1)

        @pl.when(later)
        def _():
            pl.semaphore_signal(barrier, inc=1, device_id=peer(dy, dz), device_id_type=MESH)

    for other in pair_peers:
        earlier = earlier + jnp.where(other > pair, 0, 1)

        @pl.when(other > pair)
        def _():
            pl.semaphore_signal(barrier, inc=1, device_id=(row, other), device_id_type=MESH)

    @pl.when(core == 0)
    def _():
        pl.semaphore_signal(barrier, inc=1, device_id=sibling, device_id_type=MESH)

    sa_load = pltpu.make_async_copy(sa_hbm, sa, load_sem.at[1])
    sa_load.start()
    d2_load = pltpu.make_async_copy(d2_hbm, d2, load_sem.at[2])
    d2_load.start()
    d1_load = pltpu.make_async_copy(d1_hbm, d1, load_sem.at[3])
    d1_load.start()
    kw_load = pltpu.make_async_copy(kw_hbm, kw, load_sem.at[4])
    kw_load.start()
    g_loads = []
    for p in range(2):
        for h in range(2):
            load = pltpu.make_async_copy(
                g_hbm.at[p, :, pl.ds(h * 24, 24), :], gbuf.at[p, h], load_sem.at[5 + 2 * p + h]
            )
            load.start()
            g_loads.append(load)

    kg_load.wait()
    kgbuf[0, core, 0] = jnp.concatenate([kgin[0:24, :], kgin[24:48, :]], axis=1)

    @pl.when(earlier > 0)
    def _():
        pl.semaphore_wait(barrier, earlier)

    kg_copies = {}
    for n, (dy, dz) in enumerate(SEND_ORDER):
        chunk, slot = slot_of(dy, (8 - dz) % 8)
        kg_copies[dy, dz] = pltpu.make_async_remote_copy(
            kgbuf.at[0, core, 0], kgbuf.at[chunk, core, slot], kg_send.at[n], kg_recv.at[chunk, slot],
            device_id=peer(dy, dz), device_id_type=MESH,
        )
    for dy, dz in SEND_ORDER:

        @pl.when(jnp.logical_not(is_later(dy, dz)))
        def _():
            pl.semaphore_signal(
                here.at[number(dy, (8 - dz) % 8)], inc=1, device_id=peer(dy, dz), device_id_type=MESH
            )
            kg_copies[dy, dz].start()

    @pl.when(core == 1)
    def _():
        pl.semaphore_signal(here.at[15], inc=1, device_id=sibling, device_id_type=MESH)

    for n, other in enumerate(pair_peers):

        @pl.when(other < pair)
        def _():
            pl.semaphore_signal(here.at[16 + 6 - n], inc=1, device_id=(row, other), device_id_type=MESH)

    def serve_later(places):
        for dy, dz in places:

            @pl.when(is_later(dy, dz))
            def _():
                pl.semaphore_wait(here.at[number(dy, dz)], 1)
                kg_copies[dy, dz].start()

    serve_later(NEAR[1:])

    sa_load.wait()
    high, low = split(sa[...].reshape(128, 512))
    w[0:128] = high
    w[128:256] = low
    d2_load.wait()
    cross(d2, w, s8)
    fall[core, chip] = as_row(s8)
    serve_later(FAR)
    f_copies = []
    for n, (dy, dz) in enumerate(SEND_ORDER):
        copy = pltpu.make_async_remote_copy(
            fall.at[core, chip], fall.at[core, chip], f_send.at[n], f_recv.at[n],
            device_id=peer(dy, dz), device_id_type=MESH,
        )
        copy.start()
        f_copies.append(copy)

    for load in g_loads:
        load.wait()

    def split_general(n, _):
        p, h, c = n // 4, (n // 2) % 2, n % 2
        for chunk in range(2):
            for s in range(0, 8, 2):
                first, second = (chip_at(*PLACES[chunk][s + i]) * 2 + c for i in range(2))
                both = jnp.concatenate([gbuf[p, h, first], gbuf[p, h, second]], axis=0)
                a, b = split(both)
                ghi[chunk, p, h, c, s * 24:s * 24 + 48, :] = a
                glo[chunk, p, h, c, s * 24:s * 24 + 48, :] = b
        return 0

    lax.fori_loop(0, 8, split_general, 0)

    @pl.when(core == 0)
    def _():
        pl.semaphore_wait(here.at[15], 1)

    def hand_over(chunk):
        for slot in range(8):
            if (chunk, slot) != (0, 0):
                kg_copies[tuple((8 - a) % 8 if i else a for i, a in enumerate(PLACES[chunk][slot]))].wait_recv()
        copy = pltpu.make_async_remote_copy(
            kgbuf.at[chunk, core], kgbuf.at[chunk, core], sib_send.at[chunk], sib_recv.at[chunk],
            device_id=sibling, device_id_type=MESH,
        )
        copy.start()
        return copy

    def rotate(chunk):
        x = kgbuf[chunk].reshape(384, 128).T
        high, low = split(jnp.concatenate([x[0:64], x[64:128]], axis=1))
        left[0:64] = high
        left[64:128] = low
        for p in range(2):
            gh = ghi[chunk, p].reshape(768, 512)
            gl = glo[chunk, p].reshape(768, 512)
            a = lax.dot_general(left[...], gh, PLAIN, preferred_element_type=F32)
            b = lax.dot_general(left[0:64], gl, PLAIN, preferred_element_type=F32)
            part = a[0:64] + a[64:128] + b
            moved[p] = part if chunk == 0 else moved[p] + part

    near = hand_over(0)
    near.wait_recv()
    rotate(0)
    far = hand_over(1)

    for copy in f_copies:
        copy.wait_recv()
    f_over = pltpu.make_async_remote_copy(
        fall.at[core], fall.at[core], sib_send.at[2], sib_recv.at[2], device_id=sibling, device_id_type=MESH,
    )
    f_over.start()

    far.wait_recv()
    rotate(1)
    high, low = split(moved[...].reshape(128, 512))
    w[0:128] = high
    w[128:256] = low
    cross(d2, w, s8)
    exchange = as_row(s8)

    d1_load.wait()
    high, low = split(jnp.broadcast_to(d1[...], (16, 512)))
    at = lax.broadcasted_iota(jnp.int32, (16, 512), 0)
    ones = jnp.where(at == 0, high.astype(F32), jnp.where(at == 1, low.astype(F32), 0.0)).astype(BF16)
    c = lax.dot_general(ones, w[...], ROW_BY_ROW, preferred_element_type=F32)
    c = c[0:1] + c[1:2]
    coulomb = c[:, 0:128] + c[:, 128:256]

    kw_load.wait()
    f_over.wait_recv()
    lane = lax.broadcasted_iota(jnp.int32, (1, 128), 1)
    acc = [jnp.zeros((1, 128), F32) for _ in range(2)]
    for k in range(16):
        for c in range(2):
            f = fall[c, k]
            for p in range(2):
                q = 4 * k + 2 * c
                acc[p] = acc[p] + f * jnp.where(lane < 64, kw[p, q], kw[p, q + 1])
    turned = jnp.concatenate([a[:, 0:64] + a[:, 64:128] for a in acc], axis=1)

    pbuf[pair] = exchange + 2.0 * coulomb + turned
    p_copies = []
    for n, other in enumerate(pair_peers):

        @pl.when(other > pair)
        def _():
            pl.semaphore_wait(here.at[16 + n], 1)

        copy = pltpu.make_async_remote_copy(
            pbuf.at[pair], pbuf.at[pair], p_send.at[n], p_recv.at[n], device_id=(row, other), device_id_type=MESH,
        )
        copy.start()
        p_copies.append(copy)
    for copy in p_copies:
        copy.wait_recv()
    total = pbuf[0]
    for k in range(1, 8):
        total = total + pbuf[k]
    total = 2.0 * total
    out_ref[0:1, :] = total[:, 0:64]
    out_ref[1:2, :] = total[:, 64:128]

    for copy in list(kg_copies.values()) + f_copies + p_copies + [near, far, f_over]:
        copy.wait_send()


def per_device(slab_active, slab_general, kappa_general, kappa_window, density_one, density_two):
    dma = pltpu.SemaphoreType.DMA
    return pl.pallas_call(
        kernel,
        out_shape=jax.ShapeDtypeStruct((2, 64), F32),
        in_specs=[pl.BlockSpec(memory_space=pltpu.HBM)] * 6,
        out_specs=pl.BlockSpec(memory_space=pltpu.VMEM),
        scratch_shapes=[
            pltpu.VMEM((2, 64, 512), F32),
            pltpu.VMEM((2, 2, 32, 24, 512), F32),
            pltpu.VMEM((48, 64), F32),
            pltpu.SMEM((2, 64), F32),
            pltpu.VMEM((1, 512), F32),
            pltpu.VMEM((64, 64, 512), BF16),
            pltpu.VMEM((2, 2, 2, 2, 192, 512), BF16),
            pltpu.VMEM((2, 2, 2, 2, 192, 512), BF16),
            pltpu.VMEM((2, 2, 8, 24, 128), F32),
            pltpu.VMEM((128, 768), BF16),
            pltpu.VMEM((256, 512), BF16),
            pltpu.VMEM((64, 8, 256), F32),
            pltpu.VMEM((2, 64, 512), F32),
            pltpu.VMEM((2, 16, 1, 128), F32),
            pltpu.VMEM((8, 1, 128), F32),
            dma((9,)),
            pltpu.SemaphoreType.REGULAR((23,)),
            dma((15,)),
            dma((2, 8)),
            dma((15,)),
            dma((15,)),
            dma((3,)),
            dma((3,)),
            dma((7,)),
            dma((7,)),
        ],
        compiler_params=pltpu.CompilerParams(
            collective_id=0, has_side_effects=True, vmem_limit_bytes=48 * 2**20
        ),
        name="sigma",
    )(*(
        pltpu.with_memory_space_constraint(x, pltpu.HBM)
        for x in (
            slab_active,
            slab_general.reshape(2, 32, 48, 512),
            kappa_general,
            kappa_window,
            density_one.reshape(1, 512),
            density_two,
        )
    ))


def solution(mesh):
    in_specs = (
        P("rows", None, "pairs"),
        P("rows", None, "pairs"),
        P("rows", None),
        P("rows", None),
        P("pairs"),
        P(None, None, "pairs"),
    )
    out_specs = P("rows", None)
    return jax.shard_map(
        per_device, mesh=mesh, in_specs=in_specs, out_specs=out_specs, check_vma=False
    )
```

```python
import jax
import jax.numpy as jnp
from jax import lax
from jax.experimental import pallas as pl
from jax.experimental.pallas import tpu as pltpu
from jax.sharding import PartitionSpec as P

MESH = pl.DeviceIdType.MESH
BF16, F32 = jnp.bfloat16, jnp.float32
ROW_BY_ROW = (((1,), (1,)), ((), ()))
PLAIN = (((1,), (0,)), ((), ()))

OWN = ((1, 3), (1, 2), (0, 3), (1, 1), (0, 2), (1, 0), (0, 1))
CUT = ((1, 1), (0, 1), (1, 2), (1, 0), (0, 2), (0, 0), (1, 3), (0, 3))
DIRECT = ((1, 1), (0, 1), (1, 3), (0, 3))
ALL = tuple((1, *o) for o in CUT) + tuple((0, *o) for o in OWN)


def own_slot(dy, dk):
    return dy * 4 + dk


def cut_slot(dy, dk):
    return dk * 2 + dy


def f_slot(cut, dy, dk):
    return 8 + cut_slot(dy, dk) if cut else own_slot(dy, dk)


def split(x):
    high = x.astype(BF16)
    return high, (x - high.astype(F32)).astype(BF16)


def cross(d2_ref, w_ref, s8_ref):
    sub = lax.broadcasted_iota(jnp.int32, (8, 256), 0)
    lane = lax.broadcasted_iota(jnp.int32, (8, 256), 1) % 64
    masks = [lane == sub + 8 * k for k in range(8)]
    group = 8
    for b in range(64 // group):
        r = lax.dot_general(
            d2_ref[b * group:(b + 1) * group].reshape(group * 64, 512), w_ref[...], ROW_BY_ROW,
            preferred_element_type=F32,
        )
        for t in range(group):
            acc = jnp.zeros((8, 256), F32)
            for k in range(8):
                at = (t * 8 + k) * 8
                acc = jnp.where(masks[k], r[at:at + 8, :], acc)
            s8_ref[b * group + t] = acc


def as_row(s8_ref):
    s = jnp.sum(s8_ref[...], axis=1).T
    pair = jnp.sum(s.reshape(2, 2, 64, 64), axis=(0, 2))
    return jnp.concatenate([pair[0:1], pair[1:2]], axis=1)


def kernel(
    sa_hbm, g_hbm, kg_hbm, kw_hbm, d1_hbm, d2_hbm, out_ref,
    sa, gbuf, kgin, kw, d1, d2, ghi, glo, kg, left, w, s8, moved, fall, pbuf,
    load_sem, near_here, far_here, hop_here, own_send, own_recv, cut_send, cut_recv, pass_send, pass_recv,
    sib_send, sib_recv, f_send, f_recv, p_send, p_recv,
):
    row, pair = lax.axis_index("rows"), lax.axis_index("pairs")
    core, chip = row % 2, row // 2
    ylo, z = chip // 8, chip % 8
    half, k = z // 4, z % 4
    x, yhi = pair // 2, pair % 2
    early, late = half == 0, half == 1

    def chip_of(cut, dy, dk):
        return (ylo ^ dy) * 8 + (half ^ cut) * 4 + (k ^ dk)

    def peer(cut, dy, dk):
        return (chip_of(cut, dy, dk) * 2 + core, pair)

    def signal(semaphore, device):
        pl.semaphore_signal(semaphore, inc=1, device_id=device, device_id_type=MESH)

    def remote(source, target, send, recv, device):
        return pltpu.make_async_remote_copy(
            source, target, send, recv, device_id=device, device_id_type=MESH
        )

    def is_later(dy, dk):
        return (k ^ dk) * 2 + (ylo ^ dy) > k * 2 + ylo

    sibling = (chip * 2 + 1 - core, pair)
    beside = [((chip ^ 1) * 2 + core, pair), ((chip ^ 1) * 2 + 1 - core, pair)]
    pair_peers = [lax.rem(pair + n, 8) for n in range(1, 8)]
    y = yhi * 2 + ylo

    def at(x, y, z):
        return (((y % 2) * 8 + z) * 2 + core, x * 2 + y // 2)

    hops = (
        (at((x + 1) % 4, y, z), None),
        (at((x + 3) % 4, y, z), None),
        (at(x, (y + 1) % 4, z), None),
        (at(x, (y + 3) % 4, z), None),
        (at(x, y, (z + 1) % 8), k < 3),
        (at(x, y, (z + 7) % 8), k > 0),
        (sibling, None),
    )

    def for_hops(condition, act):
        for n, (device, there) in enumerate(hops):
            @pl.when(condition if there is None else jnp.logical_and(condition, there))
            def _():
                act(n, device)

    kg_load = pltpu.make_async_copy(kg_hbm, kgin, load_sem.at[0])
    kg_load.start()

    barrier = pltpu.get_barrier_semaphore()

    @pl.when(early)
    def _():
        for dy, dk in CUT:
            signal(barrier, peer(1, dy, dk))
        for other in pair_peers:
            signal(barrier, (row, other))
        signal(barrier, sibling)
        signal(barrier, beside[1])
        for dy, dk in OWN:
            @pl.when(is_later(dy, dk))
            def _():
                signal(barrier, peer(0, dy, dk))

    for_hops(late, lambda n, device: signal(barrier, device))

    sa_load = pltpu.make_async_copy(sa_hbm, sa, load_sem.at[1])
    sa_load.start()
    d2_load = pltpu.make_async_copy(d2_hbm, d2, load_sem.at[2])
    d2_load.start()
    d1_load = pltpu.make_async_copy(d1_hbm, d1, load_sem.at[3])
    d1_load.start()
    kw_load = pltpu.make_async_copy(kw_hbm, kw, load_sem.at[4])
    kw_load.start()
    g_loads = []
    for p in range(2):
        for h in range(2):
            load = pltpu.make_async_copy(
                g_hbm.at[p, :, pl.ds(h * 24, 24), :], gbuf.at[p, h], load_sem.at[5 + 2 * p + h]
            )
            load.start()
            g_loads.append(load)

    kg_load.wait()
    kg[0, core, 0] = jnp.concatenate([kgin[0:24, :], kgin[24:48, :]], axis=1)
    pl.semaphore_wait(barrier, jnp.where(early, 9 + 2 * k + ylo, 14 + jnp.where(jnp.logical_or(k == 0, k == 3), 0, 1)))

    own = {}
    for n, (dy, dk) in enumerate(OWN):
        own[dy, dk] = remote(
            kg.at[0, core, 0], kg.at[0, core, own_slot(dy, dk)], own_send.at[n], own_recv.at[n], peer(0, dy, dk)
        )
    cut = {}
    for n, (dy, dk) in enumerate(DIRECT):
        cut[dy, dk] = remote(
            kg.at[0, core, 0], kg.at[1, core, cut_slot(dy, dk)], cut_send.at[n], cut_recv.at[n], peer(1, dy, dk)
        )

    @pl.when(late)
    def _():
        for copy in cut.values():
            copy.start()
        for n, (dy, dk) in enumerate(CUT):
            signal(far_here.at[n], peer(1, dy, dk))
        for_hops(late, lambda n, device: signal(hop_here.at[0, n ^ 1 if n < 6 else n], device))

    @pl.when(early)
    def _():
        for n, (dy, dk) in enumerate(OWN):
            @pl.when(jnp.logical_not(is_later(dy, dk)))
            def _():
                signal(near_here.at[n], peer(0, dy, dk))
                own[dy, dk].start()

    sa_load.wait()
    high, low = split(sa[...].reshape(128, 512))
    w[0:128] = high
    w[128:256] = low
    d2_load.wait()
    cross(d2, w, s8)
    fall[core, 0] = as_row(s8)
    f_copies = {}
    for n, (c, dy, dk) in enumerate(ALL):
        f_copies[c, dy, dk] = remote(
            fall.at[core, 0], fall.at[core, f_slot(c, dy, dk)], f_send.at[n], f_recv.at[n], peer(c, dy, dk)
        )

    @pl.when(late)
    def _():
        for dy, dk in CUT:
            f_copies[1, dy, dk].start()
        for step in range(3):
            for_hops(late, lambda n, device: pl.semaphore_wait(hop_here.at[step, n], 1))
            if step < 2:
                for_hops(late, lambda n, device: signal(hop_here.at[step + 1, n ^ 1 if n < 6 else n], device))
        for dy, dk in OWN:
            own[dy, dk].start()
        for dy, dk in OWN:
            f_copies[0, dy, dk].start()

    @pl.when(early)
    def _():
        for n, (dy, dk) in enumerate(OWN):
            @pl.when(is_later(dy, dk))
            def _():
                pl.semaphore_wait(near_here.at[n], 1)
                own[dy, dk].start()
        for dy, dk in OWN:
            f_copies[0, dy, dk].start()

    for load in g_loads:
        load.wait()

    def split_general(n, _):
        p, h, c = n // 4, (n // 2) % 2, n % 2
        for part, chips in ((0, [chip_of(0, i // 4, i % 4) for i in range(8)]), (1, [chip_of(1, i % 2, i // 2) for i in range(8)])):
            for s in range(0, 8, 2):
                both = jnp.concatenate([gbuf[p, h, chips[s] * 2 + c], gbuf[p, h, chips[s + 1] * 2 + c]], axis=0)
                a, b = split(both)
                ghi[part, p, h, c, s * 24:s * 24 + 48, :] = a
                glo[part, p, h, c, s * 24:s * 24 + 48, :] = b
        return 0

    lax.fori_loop(0, 8, split_general, 0)

    @pl.when(early)
    def _():
        for n, (dy, dk) in enumerate(CUT):
            pl.semaphore_wait(far_here.at[n], 1)
            if (dy, dk) in DIRECT:
                cut[dy, dk].start()
        for dy, dk in CUT:
            f_copies[1, dy, dk].start()

    passes = {}
    for n, dk in enumerate((3, 1)):
        mine = kg.at[1, core, pl.ds(2 * dk, 2)]
        theirs = kg.at[1, core, pl.ds(2 * (dk ^ 1), 2)]
        for m, (target, device) in enumerate(((theirs, beside[0]), (theirs, beside[1]), (mine, sibling))):
            passes[n, m] = remote(mine, target, pass_send.at[n, m], pass_recv.at[n, m], device)

    def pass_on():
        for n, dk in enumerate((3, 1)):
            for dy in range(2):
                cut[dy, dk].wait_recv()
            for m in range(3):
                passes[n, m].start()

    def rotate(part):
        x = kg[part].reshape(384, 128).T
        high, low = split(jnp.concatenate([x[0:64], x[64:128]], axis=1))
        left[0:64] = high
        left[64:128] = low
        result = []
        for p in range(2):
            gh = ghi[part, p].reshape(768, 512)
            gl = glo[part, p].reshape(768, 512)
            a = lax.dot_general(left[...], gh, PLAIN, preferred_element_type=F32)
            b = lax.dot_general(left[0:64], gl, PLAIN, preferred_element_type=F32)
            result.append(a[0:64] + a[64:128] + b)
        return result

    pass_on()
    for copy in own.values():
        copy.wait_recv()
    over = remote(kg.at[0, core], kg.at[0, core], sib_send.at[0], sib_recv.at[0], sibling)
    over.start()
    over.wait_recv()
    for p, part in enumerate(rotate(0)):
        moved[p] = part

    for copy in f_copies.values():
        copy.wait_recv()
    f_over = remote(fall.at[core], fall.at[core], sib_send.at[1], sib_recv.at[1], sibling)
    f_over.start()
    d1_load.wait()
    high, low = split(jnp.broadcast_to(d1[...], (16, 512)))
    line = lax.broadcasted_iota(jnp.int32, (16, 512), 0)
    ones = jnp.where(line == 0, high.astype(F32), jnp.where(line == 1, low.astype(F32), 0.0)).astype(BF16)
    kw_load.wait()
    f_over.wait_recv()
    lane = lax.broadcasted_iota(jnp.int32, (1, 128), 1)
    acc = [jnp.zeros((1, 128), F32) for _ in range(2)]
    for c, dy, dk in ((0, 0, 0),) + ALL:
        first = 4 * chip_of(c, dy, dk)
        for n in range(2):
            f = fall[n, f_slot(c, dy, dk)]
            for p in range(2):
                q = first + 2 * n
                acc[p] = acc[p] + f * jnp.where(lane < 64, kw[p, q], kw[p, q + 1])
    turned = jnp.concatenate([a[:, 0:64] + a[:, 64:128] for a in acc], axis=1)

    for copy in passes.values():
        copy.wait_recv()
    for p, part in enumerate(rotate(1)):
        high, low = split(moved[p] + part)
        w[64 * p:64 * p + 64] = high
        w[128 + 64 * p:192 + 64 * p] = low
    cross(d2, w, s8)
    exchange = as_row(s8)
    c = lax.dot_general(ones, w[...], ROW_BY_ROW, preferred_element_type=F32)
    c = c[0:1] + c[1:2]
    coulomb = c[:, 0:128] + c[:, 128:256]

    pbuf[pair] = exchange + 2.0 * coulomb + turned
    p_copies = []
    for n, other in enumerate(pair_peers):
        copy = remote(pbuf.at[pair], pbuf.at[pair], p_send.at[n], p_recv.at[n], (row, other))
        copy.start()
        p_copies.append(copy)
    for copy in p_copies:
        copy.wait_recv()
    total = pbuf[0]
    for n in range(1, 8):
        total = total + pbuf[n]
    total = 2.0 * total
    out_ref[0:1, :] = total[:, 0:64]
    out_ref[1:2, :] = total[:, 64:128]

    for copies in (own.values(), cut.values(), passes.values(), f_copies.values(), p_copies, (over, f_over)):
        for copy in copies:
            copy.wait_send()

def per_device(slab_active, slab_general, kappa_general, kappa_window, density_one, density_two):
    dma, regular = pltpu.SemaphoreType.DMA, pltpu.SemaphoreType.REGULAR
    return pl.pallas_call(
        kernel,
        out_shape=jax.ShapeDtypeStruct((2, 64), F32),
        in_specs=[pl.BlockSpec(memory_space=pltpu.HBM)] * 6,
        out_specs=pl.BlockSpec(memory_space=pltpu.VMEM),
        scratch_shapes=[
            pltpu.VMEM((2, 64, 512), F32),
            pltpu.VMEM((2, 2, 32, 24, 512), F32),
            pltpu.VMEM((48, 64), F32),
            pltpu.SMEM((2, 64), F32),
            pltpu.VMEM((1, 512), F32),
            pltpu.VMEM((64, 64, 512), BF16),
            pltpu.VMEM((2, 2, 2, 2, 192, 512), BF16),
            pltpu.VMEM((2, 2, 2, 2, 192, 512), BF16),
            pltpu.VMEM((2, 2, 8, 24, 128), F32),
            pltpu.VMEM((128, 768), BF16),
            pltpu.VMEM((256, 512), BF16),
            pltpu.VMEM((64, 8, 256), F32),
            pltpu.VMEM((2, 64, 512), F32),
            pltpu.VMEM((2, 16, 1, 128), F32),
            pltpu.VMEM((8, 1, 128), F32),
            dma((9,)),
            regular((7,)),
            regular((8,)),
            regular((3, 7)),
            dma((7,)),
            dma((7,)),
            dma((4,)),
            dma((4,)),
            dma((2, 3)),
            dma((2, 3)),
            dma((2,)),
            dma((2,)),
            dma((15,)),
            dma((15,)),
            dma((7,)),
            dma((7,)),
        ],
        compiler_params=pltpu.CompilerParams(
            collective_id=0, has_side_effects=True, vmem_limit_bytes=48 * 2**20
        ),
        name="sigma",
    )(*(
        pltpu.with_memory_space_constraint(x, pltpu.HBM)
        for x in (
            slab_active,
            slab_general.reshape(2, 32, 48, 512),
            kappa_general,
            kappa_window,
            density_one.reshape(1, 512),
            density_two,
        )
    ))


def solution(mesh):
    in_specs = (
        P("rows", None, "pairs"),
        P("rows", None, "pairs"),
        P("rows", None),
        P("rows", None),
        P("pairs"),
        P(None, None, "pairs"),
    )
    out_specs = P("rows", None)
    return jax.shard_map(
        per_device, mesh=mesh, in_specs=in_specs, out_specs=out_specs, check_vma=False
    )
```

```python
import jax
import jax.numpy as jnp
from jax import lax
from jax.experimental import pallas as pl
from jax.experimental.pallas import tpu as pltpu
from jax.sharding import PartitionSpec as P

MESH = pl.DeviceIdType.MESH
BF16, F32 = jnp.bfloat16, jnp.float32
ROW_BY_ROW = (((1,), (1,)), ((), ()))
PLAIN = (((1,), (0,)), ((), ()))

OWN = ((1, 3), (1, 2), (0, 3), (1, 1), (0, 2), (1, 0), (0, 1))
DIRECT = ((1, 1), (0, 1), (1, 3), (0, 3))


ORDER = (3, 1, 2, 0)


def own_slot(dy, dk):
    return dy * 4 + dk


def cut_slot(dy, dk):
    return ORDER.index(dk) * 2 + dy


def split(x):
    high = x.astype(BF16)
    return high, (x - high.astype(F32)).astype(BF16)


def cross(d2_ref, w_ref, s8_ref, groups=range(8)):
    sub = lax.broadcasted_iota(jnp.int32, (8, 256), 0)
    lane = lax.broadcasted_iota(jnp.int32, (8, 256), 1) % 64
    masks = [lane == sub + 8 * k for k in range(8)]
    group = 8
    for b in groups:
        r = lax.dot_general(
            d2_ref[b * group:(b + 1) * group].reshape(group * 64, 512), w_ref[...], ROW_BY_ROW,
            preferred_element_type=F32,
        )
        for t in range(group):
            acc = jnp.zeros((8, 256), F32)
            for k in range(8):
                at = (t * 8 + k) * 8
                acc = jnp.where(masks[k], r[at:at + 8, :], acc)
            s8_ref[b * group + t] = acc


def as_row(s8_ref):
    s = jnp.sum(s8_ref[...], axis=1).T
    pair = jnp.sum(s.reshape(2, 2, 64, 64), axis=(0, 2))
    return jnp.concatenate([pair[0:1], pair[1:2]], axis=1)


def kernel(
    sa_hbm, g_hbm, kg_hbm, kw_hbm, d1_hbm, d2_hbm, out_ref,
    sa, gbuf, kgin, kw, d1, d2, ghi, glo, cut_hi, cut_lo, kg, w, s8, moved, fall, pbuf,
    load_sem, near_here, far_here, pair_here, hop_here, own_send, own_recv, cut_send, cut_recv, pass_send, pass_recv,
    sib_send, sib_recv, f_send, f_recv, f_pass_send, f_pass_recv, p_send, p_recv,
):
    row, pair = lax.axis_index("rows"), lax.axis_index("pairs")
    core, chip = row % 2, row // 2
    ylo, z = chip // 8, chip % 8
    half, k = z // 4, z % 4
    x, yhi = pair // 2, pair % 2
    early, late = half == 0, half == 1

    def chip_of(cut, dy, dk):
        return (ylo ^ dy) * 8 + (half ^ cut) * 4 + (k ^ dk)

    def peer(cut, dy, dk):
        return (chip_of(cut, dy, dk) * 2 + core, pair)

    def signal(semaphore, device):
        pl.semaphore_signal(semaphore, inc=1, device_id=device, device_id_type=MESH)

    def remote(source, target, send, recv, device):
        return pltpu.make_async_remote_copy(
            source, target, send, recv, device_id=device, device_id_type=MESH
        )

    def is_later(dy, dk):
        return (k ^ dk) * 2 + (ylo ^ dy) > k * 2 + ylo

    sibling = (chip * 2 + 1 - core, pair)
    beside = [((chip ^ 1) * 2 + core, pair), ((chip ^ 1) * 2 + 1 - core, pair)]
    pair_peers = [pair ^ n for n in (5, 7, 4, 6, 3, 1, 2)]
    y = yhi * 2 + ylo

    def at(x, y, z):
        return (((y % 2) * 8 + z) * 2 + core, x * 2 + y // 2)

    hops = (
        (at((x + 1) % 4, y, z), x < 3),
        (at((x + 3) % 4, y, z), x > 0),
        (at(x, (y + 1) % 4, z), y < 3),
        (at(x, (y + 3) % 4, z), y > 0),
        (at(x, y, (z + 1) % 8), k < 3),
        (at(x, y, (z + 7) % 8), k > 0),
        (sibling, None),
    )

    def for_hops(condition, act):
        for n, (device, there) in enumerate(hops):
            @pl.when(condition if there is None else jnp.logical_and(condition, there))
            def _():
                act(n, device)

    kg_load = pltpu.make_async_copy(kg_hbm, kgin, load_sem.at[0])
    kg_load.start()

    barrier = pltpu.get_barrier_semaphore()

    def is_later_pair(other):
        return (other % 2) * 4 + other // 2 > yhi * 4 + x

    @pl.when(early)
    def _():
        for dy, dk in DIRECT:
            signal(barrier, peer(1, dy, dk))
        for dy, dk in OWN:
            @pl.when(is_later(dy, dk))
            def _():
                signal(barrier, peer(0, dy, dk))
        for other in pair_peers:
            @pl.when(is_later_pair(other))
            def _():
                signal(barrier, (row, other))
        signal(barrier, sibling)
        @pl.when(k % 2 == 0)
        def _():
            signal(barrier, beside[1])

    for_hops(late, lambda n, device: signal(barrier, device))

    sa_load = pltpu.make_async_copy(sa_hbm, sa, load_sem.at[1])
    sa_load.start()
    d2_load = pltpu.make_async_copy(d2_hbm, d2, load_sem.at[2])
    d2_load.start()
    d1_load = pltpu.make_async_copy(d1_hbm, d1, load_sem.at[3])
    d1_load.start()
    kw_load = pltpu.make_async_copy(kw_hbm, kw, load_sem.at[4])
    kw_load.start()
    g_loads = []
    for p in range(2):
        for h in range(2):
            load = pltpu.make_async_copy(
                g_hbm.at[p, :, pl.ds(h * 24, 24), :], gbuf.at[p, h], load_sem.at[5 + 2 * p + h]
            )
            g_loads.append(load)

    kg_load.wait()
    kg[0, core, 0] = jnp.concatenate([kgin[0:24, :], kgin[24:48, :]], axis=1)

    def inner(v):
        return jnp.where(jnp.logical_or(v == 0, v == 3), 0, 1)

    pl.semaphore_wait(
        barrier, jnp.where(early, 1 + 2 * k + ylo + 4 * yhi + x + k % 2, 8 + inner(x) + inner(y) + inner(k))
    )

    own = {}
    for n, (dy, dk) in enumerate(OWN):
        own[dy, dk] = remote(
            kg.at[0, core, 0], kg.at[0, core, own_slot(dy, dk)], own_send.at[n], own_recv.at[n], peer(0, dy, dk)
        )
    cut = {}
    for n, (dy, dk) in enumerate(DIRECT):
        cut[dy, dk] = remote(
            kg.at[0, core, 0], kg.at[1, core, cut_slot(dy, dk)], cut_send.at[n], cut_recv.at[n], peer(1, dy, dk)
        )

    @pl.when(late)
    def _():
        for copy in cut.values():
            copy.start()
        for n, (dy, dk) in enumerate(DIRECT):
            signal(far_here.at[n], peer(1, dy, dk))
        for_hops(late, lambda n, device: signal(hop_here.at[0, n ^ 1 if n < 6 else n], device))

    @pl.when(early)
    def _():
        for n, (dy, dk) in enumerate(OWN):
            @pl.when(jnp.logical_not(is_later(dy, dk)))
            def _():
                signal(near_here.at[n], peer(0, dy, dk))
                own[dy, dk].start()
        for n, other in enumerate(pair_peers):
            @pl.when(jnp.logical_not(is_later_pair(other)))
            def _():
                signal(pair_here.at[n], (row, other))
        @pl.when(k % 2 == 1)
        def _():
            signal(pair_here.at[7], beside[1])

    def next_round(step):
        for_hops(late, lambda n, device: pl.semaphore_wait(hop_here.at[step, n], 1))
        if step < 3:
            for_hops(late, lambda n, device: signal(hop_here.at[step + 1, n ^ 1 if n < 6 else n], device))

    sa_load.wait()
    high, low = split(sa[...].reshape(128, 512))
    w[0:128] = high
    w[128:256] = low
    d2_load.wait()
    for load in g_loads:
        load.start()
    cross(d2, w, s8, range(4))
    next_round(0)
    cross(d2, w, s8, range(4, 8))
    fall[0, core, 0] = as_row(s8)
    next_round(1)
    f_own = {}
    for n, (dy, dk) in enumerate(OWN):
        f_own[dy, dk] = remote(
            fall.at[0, core, 0], fall.at[0, core, own_slot(dy, dk)], f_send.at[n], f_recv.at[n], peer(0, dy, dk)
        )
    f_cut = {}
    for n, (dy, dk) in enumerate(DIRECT):
        f_cut[dy, dk] = remote(
            fall.at[0, core, 0], fall.at[1, core, cut_slot(dy, dk)], f_send.at[7 + n], f_recv.at[7 + n], peer(1, dy, dk)
        )

    @pl.when(late)
    def _():
        for copy in f_cut.values():
            copy.start()
        next_round(2)
        for dy, dk in OWN:
            own[dy, dk].start()
        for copy in f_own.values():
            copy.start()

    @pl.when(early)
    def _():
        for n, (dy, dk) in enumerate(OWN):
            @pl.when(is_later(dy, dk))
            def _():
                pl.semaphore_wait(near_here.at[n], 1)
                own[dy, dk].start()
        for copy in f_own.values():
            copy.start()

    for load in g_loads:
        load.wait()

    def split_general(n, _):
        p, h, c = n // 4, (n // 2) % 2, n % 2

        def put(high, low, chips):
            for s in range(0, len(chips), 2):
                a, b = split(jnp.concatenate([gbuf[p, h, chips[s + i] * 2 + c] for i in range(2)], axis=0))
                high[s * 24:s * 24 + 48, :] = a
                low[s * 24:s * 24 + 48, :] = b

        put(ghi.at[p, h, c], glo.at[p, h, c], [chip_of(0, s // 4, s % 4) for s in range(8)])
        for part in range(2):
            chips = [chip_of(1, s % 2, ORDER[s // 2]) for s in range(4 * part, 4 * part + 4)]
            put(cut_hi.at[part, p, h, c], cut_lo.at[part, p, h, c], chips)
        return 0

    lax.fori_loop(0, 8, split_general, 0)

    @pl.when(early)
    def _():
        for n, (dy, dk) in enumerate(DIRECT):
            pl.semaphore_wait(far_here.at[n], 1)
            cut[dy, dk].start()
        for copy in f_cut.values():
            copy.start()

    @pl.when(jnp.logical_and(early, k % 2 == 0))
    def _():
        pl.semaphore_wait(pair_here.at[7], 1)


    def handed_on(array, send, recv):
        copies = {}
        for n, dk in enumerate((3, 1)):
            mine = array.at[1, core, pl.ds(cut_slot(0, dk), 2)]
            theirs = array.at[1, core, pl.ds(cut_slot(0, dk ^ 1), 2)]
            for m, (target, device) in enumerate(((theirs, beside[0]), (theirs, beside[1]), (mine, sibling))):
                copies[n, m] = remote(mine, target, send.at[n, m], recv.at[n, m], device)
        return copies

    def hand_on(arriving, copies):
        for n, dk in enumerate((3, 1)):
            for dy in range(2):
                arriving[dy, dk].wait_recv()
            for m in range(3):
                copies[n, m].start()

    passes = handed_on(kg, pass_send, pass_recv)
    f_passes = handed_on(fall, f_pass_send, f_pass_recv)

    def rotate(blocks, high_of, low_of):
        rows = blocks.reshape(-1, 128)
        depth = 2 * rows.shape[0]
        x = rows.T
        high, low = split(jnp.concatenate([x[0:64], x[64:128]], axis=1))
        both = jnp.concatenate([high, low], axis=0)
        result = []
        for p in range(2):
            a = lax.dot_general(both, high_of(p).reshape(depth, 512), PLAIN, preferred_element_type=F32)
            b = lax.dot_general(high, low_of(p).reshape(depth, 512), PLAIN, preferred_element_type=F32)
            result.append(a[0:64] + a[64:128] + b)
        return result

    def rotate_cut(part):
        return rotate(kg[1, :, 4 * part:4 * part + 4], lambda p: cut_hi[part, p], lambda p: cut_lo[part, p])

    hand_on(cut, passes)
    for copy in own.values():
        copy.wait_recv()
    over = remote(kg.at[0, core], kg.at[0, core], sib_send.at[0], sib_recv.at[0], sibling)
    over.start()
    over.wait_recv()
    for p, part in enumerate(rotate(kg[0], lambda p: ghi[p], lambda p: glo[p])):
        moved[p] = part
    for n in range(2):
        passes[n, 2].wait_recv()
    for p, part in enumerate(rotate_cut(0)):
        moved[p] = moved[p] + part

    for copy in f_own.values():
        copy.wait_recv()
    f_over = remote(fall.at[0, core], fall.at[0, core], sib_send.at[1], sib_recv.at[1], sibling)
    f_over.start()
    hand_on(f_cut, f_passes)
    d1_load.wait()
    high, low = split(jnp.broadcast_to(d1[...], (16, 512)))
    line = lax.broadcasted_iota(jnp.int32, (16, 512), 0)
    ones = jnp.where(line == 0, high.astype(F32), jnp.where(line == 1, low.astype(F32), 0.0)).astype(BF16)
    for n in range(2):
        for m in range(2):
            passes[n, m].wait_recv()
    for p, part in enumerate(rotate_cut(1)):
        high, low = split(moved[p] + part)
        w[64 * p:64 * p + 64] = high
        w[128 + 64 * p:192 + 64 * p] = low
    cross(d2, w, s8)
    exchange = as_row(s8)
    c = lax.dot_general(ones, w[...], ROW_BY_ROW, preferred_element_type=F32)
    c = c[0:1] + c[1:2]
    coulomb = c[:, 0:128] + c[:, 128:256]

    kw_load.wait()
    f_over.wait_recv()
    for copy in f_passes.values():
        copy.wait_recv()
    lane = lax.broadcasted_iota(jnp.int32, (1, 128), 1)
    acc = [jnp.zeros((1, 128), F32) for _ in range(2)]
    for part in range(2):
        for slot in range(8):
            first = 4 * (chip_of(1, slot % 2, ORDER[slot // 2]) if part else chip_of(0, slot // 4, slot % 4))
            for c in range(2):
                f = fall[part, c, slot]
                q = first + 2 * c
                for p in range(2):
                    acc[p] = acc[p] + f * jnp.where(lane < 64, kw[p, q], kw[p, q + 1])
    turned = jnp.concatenate([a[:, 0:64] + a[:, 64:128] for a in acc], axis=1)

    next_round(3)
    pbuf[pair] = exchange + 2.0 * coulomb + turned
    p_copies = []
    for n, other in enumerate(pair_peers):
        @pl.when(jnp.logical_and(early, is_later_pair(other)))
        def _():
            pl.semaphore_wait(pair_here.at[n], 1)

        copy = remote(pbuf.at[pair], pbuf.at[pair], p_send.at[n], p_recv.at[n], (row, other))
        copy.start()
        p_copies.append(copy)
    for copies in (own.values(), cut.values(), passes.values(), f_own.values(), f_cut.values(), f_passes.values(), (over, f_over)):
        for copy in copies:
            copy.wait_send()
    for copy in p_copies:
        copy.wait_recv()
    total = pbuf[0]
    for n in range(1, 8):
        total = total + pbuf[n]
    total = 2.0 * total
    out_ref[0:1, :] = total[:, 0:64]
    out_ref[1:2, :] = total[:, 64:128]
    for copy in p_copies:
        copy.wait_send()


def per_device(slab_active, slab_general, kappa_general, kappa_window, density_one, density_two):
    dma, regular = pltpu.SemaphoreType.DMA, pltpu.SemaphoreType.REGULAR
    return pl.pallas_call(
        kernel,
        out_shape=jax.ShapeDtypeStruct((2, 64), F32),
        in_specs=[pl.BlockSpec(memory_space=pltpu.HBM)] * 6,
        out_specs=pl.BlockSpec(memory_space=pltpu.VMEM),
        scratch_shapes=[
            pltpu.VMEM((2, 64, 512), F32),
            pltpu.VMEM((2, 2, 32, 24, 512), F32),
            pltpu.VMEM((48, 64), F32),
            pltpu.SMEM((2, 64), F32),
            pltpu.VMEM((1, 512), F32),
            pltpu.VMEM((64, 64, 512), BF16),
            pltpu.VMEM((2, 2, 2, 192, 512), BF16),
            pltpu.VMEM((2, 2, 2, 192, 512), BF16),
            pltpu.VMEM((2, 2, 2, 2, 96, 512), BF16),
            pltpu.VMEM((2, 2, 2, 2, 96, 512), BF16),
            pltpu.VMEM((2, 2, 8, 24, 128), F32),
            pltpu.VMEM((256, 512), BF16),
            pltpu.VMEM((64, 8, 256), F32),
            pltpu.VMEM((2, 64, 512), F32),
            pltpu.VMEM((2, 2, 8, 1, 128), F32),
            pltpu.VMEM((8, 1, 128), F32),
            dma((9,)),
            regular((7,)),
            regular((4,)),
            regular((8,)),
            regular((4, 7)),
            dma((7,)),
            dma((7,)),
            dma((4,)),
            dma((4,)),
            dma((2, 3)),
            dma((2, 3)),
            dma((2,)),
            dma((2,)),
            dma((11,)),
            dma((11,)),
            dma((2, 3)),
            dma((2, 3)),
            dma((7,)),
            dma((7,)),
        ],
        compiler_params=pltpu.CompilerParams(
            collective_id=0, has_side_effects=True, vmem_limit_bytes=48 * 2**20
        ),
        name="sigma",
    )(*(
        pltpu.with_memory_space_constraint(x, pltpu.HBM)
        for x in (
            slab_active,
            slab_general.reshape(2, 32, 48, 512),
            kappa_general,
            kappa_window,
            density_one.reshape(1, 512),
            density_two,
        )
    ))


def solution(mesh):
    in_specs = (
        P("rows", None, "pairs"),
        P("rows", None, "pairs"),
        P("rows", None),
        P("rows", None),
        P("pairs"),
        P(None, None, "pairs"),
    )
    out_specs = P("rows", None)
    return jax.shard_map(
        per_device, mesh=mesh, in_specs=in_specs, out_specs=out_specs, check_vma=False
    )
```

```python
import jax
import jax.numpy as jnp
from jax import lax
from jax.experimental import pallas as pl
from jax.experimental.pallas import tpu as pltpu
from jax.sharding import PartitionSpec as P

MESH = pl.DeviceIdType.MESH
BF16, F32 = jnp.bfloat16, jnp.float32
ROW_BY_ROW = (((1,), (1,)), ((), ()))
PLAIN = (((1,), (0,)), ((), ()))

OWN = ((1, 3), (1, 2), (0, 3), (1, 1), (0, 2), (1, 0), (0, 1))
DIRECT = ((1, 1), (0, 1), (1, 3), (0, 3))


ORDER = (3, 1, 2, 0)


def own_slot(dy, dk):
    return dy * 4 + dk


def cut_slot(dy, dk):
    return ORDER.index(dk) * 2 + dy


def split(x):
    high = x.astype(BF16)
    return high, (x - high.astype(F32)).astype(BF16)


def cross(d2_ref, w_ref, s8_ref, groups=range(8)):
    sub = lax.broadcasted_iota(jnp.int32, (8, 256), 0)
    lane = lax.broadcasted_iota(jnp.int32, (8, 256), 1) % 64
    masks = [lane == sub + 8 * k for k in range(8)]
    group = 8
    for b in groups:
        r = lax.dot_general(
            d2_ref[b * group:(b + 1) * group].reshape(group * 64, 512), w_ref[...], ROW_BY_ROW,
            preferred_element_type=F32,
        )
        for t in range(group):
            acc = jnp.zeros((8, 256), F32)
            for k in range(8):
                at = (t * 8 + k) * 8
                acc = jnp.where(masks[k], r[at:at + 8, :], acc)
            s8_ref[b * group + t] = acc


def as_row(s8_ref):
    s = jnp.sum(s8_ref[...], axis=1).T
    pair = jnp.sum(s.reshape(2, 2, 64, 64), axis=(0, 2))
    return jnp.concatenate([pair[0:1], pair[1:2]], axis=1)


def kernel(
    sa_hbm, g_hbm, kg_hbm, kw_hbm, d1_hbm, d2_hbm, out_ref,
    sa, gbuf, kgin, kw, d1, d2, ghi, glo, cut_hi, cut_lo, kg, w, s8, moved, fall, pbuf,
    load_sem, near_here, far_here, pair_here, hop_here, own_send, own_recv, cut_send, cut_recv, pass_send, pass_recv,
    sib_send, sib_recv, f_send, f_recv, f_pass_send, f_pass_recv, p_send, p_recv,
):
    row, pair = lax.axis_index("rows"), lax.axis_index("pairs")
    core, chip = row % 2, row // 2
    ylo, z = chip // 8, chip % 8
    half, k = z // 4, z % 4
    x, yhi = pair // 2, pair % 2
    early, late = half == 0, half == 1

    def chip_of(cut, dy, dk):
        return (ylo ^ dy) * 8 + (half ^ cut) * 4 + (k ^ dk)

    def peer(cut, dy, dk):
        return (chip_of(cut, dy, dk) * 2 + core, pair)

    def signal(semaphore, device):
        pl.semaphore_signal(semaphore, inc=1, device_id=device, device_id_type=MESH)

    def remote(source, target, send, recv, device):
        return pltpu.make_async_remote_copy(
            source, target, send, recv, device_id=device, device_id_type=MESH
        )

    def is_later(dy, dk):
        return (k ^ dk) * 2 + (ylo ^ dy) > k * 2 + ylo

    sibling = (chip * 2 + 1 - core, pair)
    beside = [((chip ^ 1) * 2 + core, pair), ((chip ^ 1) * 2 + 1 - core, pair)]
    pair_peers = [pair ^ n for n in (5, 7, 4, 6, 3, 1, 2)]
    y = yhi * 2 + ylo

    def at(x, y, z):
        return (((y % 2) * 8 + z) * 2 + core, x * 2 + y // 2)

    hops = (
        (at((x + 1) % 4, y, z), x < 3),
        (at((x + 3) % 4, y, z), x > 0),
        (at(x, (y + 1) % 4, z), y < 3),
        (at(x, (y + 3) % 4, z), y > 0),
        (at(x, y, (z + 1) % 8), k < 3),
        (at(x, y, (z + 7) % 8), k > 0),
        (sibling, None),
    )

    def for_hops(condition, act):
        for n, (device, there) in enumerate(hops):
            @pl.when(condition if there is None else jnp.logical_and(condition, there))
            def _():
                act(n, device)

    kg_load = pltpu.make_async_copy(kg_hbm, kgin, load_sem.at[0])
    kg_load.start()

    barrier = pltpu.get_barrier_semaphore()

    def is_later_pair(other):
        return (other % 2) * 4 + other // 2 > yhi * 4 + x

    @pl.when(early)
    def _():
        for dy, dk in DIRECT:
            signal(barrier, peer(1, dy, dk))
        for dy, dk in OWN:
            @pl.when(is_later(dy, dk))
            def _():
                signal(barrier, peer(0, dy, dk))
        for other in pair_peers:
            @pl.when(is_later_pair(other))
            def _():
                signal(barrier, (row, other))
        signal(barrier, sibling)
        @pl.when(k % 2 == 0)
        def _():
            signal(barrier, beside[1])

    for_hops(late, lambda n, device: signal(barrier, device))

    sa_load = pltpu.make_async_copy(sa_hbm, sa, load_sem.at[1])
    sa_load.start()
    d2_load = pltpu.make_async_copy(d2_hbm, d2, load_sem.at[2])
    d2_load.start()
    d1_load = pltpu.make_async_copy(d1_hbm, d1, load_sem.at[3])
    d1_load.start()
    kw_load = pltpu.make_async_copy(kw_hbm, kw, load_sem.at[4])
    kw_load.start()
    g_loads = []
    for p in range(2):
        for h in range(2):
            load = pltpu.make_async_copy(
                g_hbm.at[p, :, pl.ds(h * 24, 24), :], gbuf.at[p, h], load_sem.at[5 + 2 * p + h]
            )
            g_loads.append(load)

    kg_load.wait()
    kg[0, core, 0] = jnp.concatenate([kgin[0:24, :], kgin[24:48, :]], axis=1)

    def inner(v):
        return jnp.where(jnp.logical_or(v == 0, v == 3), 0, 1)

    pl.semaphore_wait(
        barrier, jnp.where(early, 1 + 2 * k + ylo + 4 * yhi + x + k % 2, 8 + inner(x) + inner(y) + inner(k))
    )

    own = {}
    for n, (dy, dk) in enumerate(OWN):
        own[dy, dk] = remote(
            kg.at[0, core, 0], kg.at[0, core, own_slot(dy, dk)], own_send.at[n], own_recv.at[n], peer(0, dy, dk)
        )
    cut = {}
    for n, (dy, dk) in enumerate(DIRECT):
        cut[dy, dk] = remote(
            kg.at[0, core, 0], kg.at[1, core, cut_slot(dy, dk)], cut_send.at[n], cut_recv.at[n], peer(1, dy, dk)
        )

    @pl.when(late)
    def _():
        for copy in cut.values():
            copy.start()
        for n, (dy, dk) in enumerate(DIRECT):
            signal(far_here.at[n], peer(1, dy, dk))
        for_hops(late, lambda n, device: signal(hop_here.at[0, n ^ 1 if n < 6 else n], device))

    @pl.when(early)
    def _():
        for n, (dy, dk) in enumerate(OWN):
            @pl.when(jnp.logical_not(is_later(dy, dk)))
            def _():
                signal(near_here.at[n], peer(0, dy, dk))
                own[dy, dk].start()
        for n, other in enumerate(pair_peers):
            @pl.when(jnp.logical_not(is_later_pair(other)))
            def _():
                signal(pair_here.at[n], (row, other))
        @pl.when(k % 2 == 1)
        def _():
            signal(pair_here.at[7], beside[1])

    def next_round(step):
        for_hops(late, lambda n, device: pl.semaphore_wait(hop_here.at[step, n], 1))
        if step < 3:
            for_hops(late, lambda n, device: signal(hop_here.at[step + 1, n ^ 1 if n < 6 else n], device))

    sa_load.wait()
    high, low = split(sa[...].reshape(128, 512))
    w[0:128] = high
    w[128:256] = low
    d2_load.wait()
    for load in g_loads:
        load.start()
    cross(d2, w, s8, range(4))
    next_round(0)
    cross(d2, w, s8, range(4, 8))
    fall[0, core, 0] = as_row(s8)
    next_round(1)
    f_own = {}
    for n, (dy, dk) in enumerate(OWN):
        f_own[dy, dk] = remote(
            fall.at[0, core, 0], fall.at[0, core, own_slot(dy, dk)], f_send.at[n], f_recv.at[n], peer(0, dy, dk)
        )
    f_cut = {}
    for n, (dy, dk) in enumerate(DIRECT):
        f_cut[dy, dk] = remote(
            fall.at[0, core, 0], fall.at[1, core, cut_slot(dy, dk)], f_send.at[7 + n], f_recv.at[7 + n], peer(1, dy, dk)
        )

    @pl.when(late)
    def _():
        for copy in f_cut.values():
            copy.start()
        next_round(2)
        for dy, dk in OWN:
            own[dy, dk].start()
        for copy in f_own.values():
            copy.start()

    @pl.when(early)
    def _():
        for n, (dy, dk) in enumerate(OWN):
            @pl.when(is_later(dy, dk))
            def _():
                pl.semaphore_wait(near_here.at[n], 1)
                own[dy, dk].start()
        for copy in f_own.values():
            copy.start()

    for load in g_loads:
        load.wait()

    def split_general(n, _):
        p, h, c = n // 4, (n // 2) % 2, n % 2

        def put(high, low, chips):
            for s in range(0, len(chips), 2):
                a, b = split(jnp.concatenate([gbuf[p, h, chips[s + i] * 2 + c] for i in range(2)], axis=0))
                high[s * 24:s * 24 + 48, :] = a
                low[s * 24:s * 24 + 48, :] = b

        put(ghi.at[p, h, c], glo.at[p, h, c], [chip_of(0, s // 4, s % 4) for s in range(8)])
        for part in range(2):
            chips = [chip_of(1, s % 2, ORDER[s // 2]) for s in range(4 * part, 4 * part + 4)]
            put(cut_hi.at[part, p, h, c], cut_lo.at[part, p, h, c], chips)
        return 0

    lax.fori_loop(0, 8, split_general, 0)

    @pl.when(early)
    def _():
        for n, (dy, dk) in enumerate(DIRECT):
            pl.semaphore_wait(far_here.at[n], 1)
            cut[dy, dk].start()
        for copy in f_cut.values():
            copy.start()

    @pl.when(jnp.logical_and(early, k % 2 == 0))
    def _():
        pl.semaphore_wait(pair_here.at[7], 1)


    def handed_on(array, send, recv):
        copies = {}
        for n, dk in enumerate((3, 1)):
            mine = array.at[1, core, pl.ds(cut_slot(0, dk), 2)]
            theirs = array.at[1, core, pl.ds(cut_slot(0, dk ^ 1), 2)]
            for m, (target, device) in enumerate(((theirs, beside[0]), (theirs, beside[1]), (mine, sibling))):
                copies[n, m] = remote(mine, target, send.at[n, m], recv.at[n, m], device)
        return copies

    def hand_on(arriving, copies):
        for n, dk in enumerate((3, 1)):
            for dy in range(2):
                arriving[dy, dk].wait_recv()
            for m in range(3):
                copies[n, m].start()

    passes = handed_on(kg, pass_send, pass_recv)
    f_passes = handed_on(fall, f_pass_send, f_pass_recv)

    def rotate(blocks, high_of, low_of):
        rows = blocks.reshape(-1, 128)
        depth = 2 * rows.shape[0]
        x = rows.T
        high, low = split(jnp.concatenate([x[0:64], x[64:128]], axis=1))
        both = jnp.concatenate([high, low], axis=0)
        result = []
        for p in range(2):
            a = lax.dot_general(both, high_of(p).reshape(depth, 512), PLAIN, preferred_element_type=F32)
            b = lax.dot_general(high, low_of(p).reshape(depth, 512), PLAIN, preferred_element_type=F32)
            result.append(a[0:64] + a[64:128] + b)
        return result

    def rotate_cut(part):
        return rotate(kg[1, :, 4 * part:4 * part + 4], lambda p: cut_hi[part, p], lambda p: cut_lo[part, p])

    hand_on(cut, passes)
    for copy in own.values():
        copy.wait_recv()
    over = remote(kg.at[0, core], kg.at[0, core], sib_send.at[0], sib_recv.at[0], sibling)
    over.start()
    over.wait_recv()
    for p, part in enumerate(rotate(kg[0], lambda p: ghi[p], lambda p: glo[p])):
        moved[p] = part

    for copy in f_own.values():
        copy.wait_recv()
    f_over = remote(fall.at[0, core], fall.at[0, core], sib_send.at[1], sib_recv.at[1], sibling)
    f_over.start()
    hand_on(f_cut, f_passes)
    for n in range(2):
        passes[n, 2].wait_recv()
    for p, part in enumerate(rotate_cut(0)):
        moved[p] = moved[p] + part
    d1_load.wait()
    high, low = split(jnp.broadcast_to(d1[...], (16, 512)))
    line = lax.broadcasted_iota(jnp.int32, (16, 512), 0)
    ones = jnp.where(line == 0, high.astype(F32), jnp.where(line == 1, low.astype(F32), 0.0)).astype(BF16)
    for n in range(2):
        for m in range(2):
            passes[n, m].wait_recv()
    for p, part in enumerate(rotate_cut(1)):
        high, low = split(moved[p] + part)
        w[64 * p:64 * p + 64] = high
        w[128 + 64 * p:192 + 64 * p] = low
    cross(d2, w, s8)
    exchange = as_row(s8)
    c = lax.dot_general(ones, w[...], ROW_BY_ROW, preferred_element_type=F32)
    c = c[0:1] + c[1:2]
    coulomb = c[:, 0:128] + c[:, 128:256]

    kw_load.wait()
    f_over.wait_recv()
    for copy in f_passes.values():
        copy.wait_recv()
    lane = lax.broadcasted_iota(jnp.int32, (1, 128), 1)
    acc = [jnp.zeros((1, 128), F32) for _ in range(2)]
    for part in range(2):
        for slot in range(8):
            first = 4 * (chip_of(1, slot % 2, ORDER[slot // 2]) if part else chip_of(0, slot // 4, slot % 4))
            for c in range(2):
                f = fall[part, c, slot]
                q = first + 2 * c
                for p in range(2):
                    acc[p] = acc[p] + f * jnp.where(lane < 64, kw[p, q], kw[p, q + 1])
    turned = jnp.concatenate([a[:, 0:64] + a[:, 64:128] for a in acc], axis=1)

    next_round(3)
    pbuf[pair] = exchange + 2.0 * coulomb + turned
    p_copies = []
    for n, other in enumerate(pair_peers):
        @pl.when(jnp.logical_and(early, is_later_pair(other)))
        def _():
            pl.semaphore_wait(pair_here.at[n], 1)

        copy = remote(pbuf.at[pair], pbuf.at[pair], p_send.at[n], p_recv.at[n], (row, other))
        copy.start()
        p_copies.append(copy)
    for copies in (own.values(), cut.values(), passes.values(), f_own.values(), f_cut.values(), f_passes.values(), (over, f_over)):
        for copy in copies:
            copy.wait_send()
    for copy in p_copies:
        copy.wait_recv()
    total = pbuf[0]
    for n in range(1, 8):
        total = total + pbuf[n]
    total = 2.0 * total
    out_ref[0:1, :] = total[:, 0:64]
    out_ref[1:2, :] = total[:, 64:128]
    for copy in p_copies:
        copy.wait_send()


def per_device(slab_active, slab_general, kappa_general, kappa_window, density_one, density_two):
    dma, regular = pltpu.SemaphoreType.DMA, pltpu.SemaphoreType.REGULAR
    return pl.pallas_call(
        kernel,
        out_shape=jax.ShapeDtypeStruct((2, 64), F32),
        in_specs=[pl.BlockSpec(memory_space=pltpu.HBM)] * 6,
        out_specs=pl.BlockSpec(memory_space=pltpu.VMEM),
        scratch_shapes=[
            pltpu.VMEM((2, 64, 512), F32),
            pltpu.VMEM((2, 2, 32, 24, 512), F32),
            pltpu.VMEM((48, 64), F32),
            pltpu.SMEM((2, 64), F32),
            pltpu.VMEM((1, 512), F32),
            pltpu.VMEM((64, 64, 512), BF16),
            pltpu.VMEM((2, 2, 2, 192, 512), BF16),
            pltpu.VMEM((2, 2, 2, 192, 512), BF16),
            pltpu.VMEM((2, 2, 2, 2, 96, 512), BF16),
            pltpu.VMEM((2, 2, 2, 2, 96, 512), BF16),
            pltpu.VMEM((2, 2, 8, 24, 128), F32),
            pltpu.VMEM((256, 512), BF16),
            pltpu.VMEM((64, 8, 256), F32),
            pltpu.VMEM((2, 64, 512), F32),
            pltpu.VMEM((2, 2, 8, 1, 128), F32),
            pltpu.VMEM((8, 1, 128), F32),
            dma((9,)),
            regular((7,)),
            regular((4,)),
            regular((8,)),
            regular((4, 7)),
            dma((7,)),
            dma((7,)),
            dma((4,)),
            dma((4,)),
            dma((2, 3)),
            dma((2, 3)),
            dma((2,)),
            dma((2,)),
            dma((11,)),
            dma((11,)),
            dma((2, 3)),
            dma((2, 3)),
            dma((7,)),
            dma((7,)),
        ],
        compiler_params=pltpu.CompilerParams(
            collective_id=0, has_side_effects=True, vmem_limit_bytes=48 * 2**20
        ),
        name="sigma",
    )(*(
        pltpu.with_memory_space_constraint(x, pltpu.HBM)
        for x in (
            slab_active,
            slab_general.reshape(2, 32, 48, 512),
            kappa_general,
            kappa_window,
            density_one.reshape(1, 512),
            density_two,
        )
    ))


def solution(mesh):
    in_specs = (
        P("rows", None, "pairs"),
        P("rows", None, "pairs"),
        P("rows", None),
        P("rows", None),
        P("pairs"),
        P(None, None, "pairs"),
    )
    out_specs = P("rows", None)
    return jax.shard_map(
        per_device, mesh=mesh, in_specs=in_specs, out_specs=out_specs, check_vma=False
    )
```

```python
import jax
import jax.numpy as jnp
from jax import lax
from jax.experimental import pallas as pl
from jax.experimental.pallas import tpu as pltpu
from jax.sharding import PartitionSpec as P

MESH = pl.DeviceIdType.MESH
BF16, F32 = jnp.bfloat16, jnp.float32
ROW_BY_ROW = (((1,), (1,)), ((), ()))
PLAIN = (((1,), (0,)), ((), ()))

OWN = ((1, 3), (1, 2), (0, 3), (1, 1), (0, 2), (1, 0), (0, 1))
DIRECT = ((1, 1), (0, 1), (1, 3), (0, 3))


ORDER = (3, 1, 2, 0)


def own_slot(dy, dk):
    return dy * 4 + dk


def cut_slot(dy, dk):
    return ORDER.index(dk) * 2 + dy


def split(x):
    high = x.astype(BF16)
    return high, (x - high.astype(F32)).astype(BF16)


def cross(d2_ref, w_ref, s8_ref, groups=range(8)):
    sub = lax.broadcasted_iota(jnp.int32, (8, 256), 0)
    lane = lax.broadcasted_iota(jnp.int32, (8, 256), 1) % 64
    masks = [lane == sub + 8 * k for k in range(8)]
    group = 8
    for b in groups:
        r = lax.dot_general(
            d2_ref[b * group:(b + 1) * group].reshape(group * 64, 512), w_ref[...], ROW_BY_ROW,
            preferred_element_type=F32,
        )
        for t in range(group):
            acc = jnp.zeros((8, 256), F32)
            for k in range(8):
                at = (t * 8 + k) * 8
                acc = jnp.where(masks[k], r[at:at + 8, :], acc)
            s8_ref[b * group + t] = acc


def as_row(s8_ref):
    s = jnp.sum(s8_ref[...], axis=1).T
    pair = jnp.sum(s.reshape(2, 2, 64, 64), axis=(0, 2))
    return jnp.concatenate([pair[0:1], pair[1:2]], axis=1)


def kernel(
    sa_hbm, g_hbm, kg_hbm, kw_hbm, d1_hbm, d2_hbm, out_ref,
    sa, gbuf, kgin, kw, d1, d2, ghi, glo, cut_hi, cut_lo, kg, w, s8, moved, fall, pbuf,
    load_sem, near_here, far_here, pair_here, hop_here, own_send, own_recv, cut_send, cut_recv, pass_send, pass_recv,
    sib_send, sib_recv, f_send, f_recv, f_pass_send, f_pass_recv, p_send, p_recv,
):
    row, pair = lax.axis_index("rows"), lax.axis_index("pairs")
    core, chip = row % 2, row // 2
    ylo, z = chip // 8, chip % 8
    half, k = z // 4, z % 4
    x, yhi = pair // 2, pair % 2
    early, late = half == 0, half == 1

    def chip_of(cut, dy, dk):
        return (ylo ^ dy) * 8 + (half ^ cut) * 4 + (k ^ dk)

    def peer(cut, dy, dk):
        return (chip_of(cut, dy, dk) * 2 + core, pair)

    def signal(semaphore, device):
        pl.semaphore_signal(semaphore, inc=1, device_id=device, device_id_type=MESH)

    def remote(source, target, send, recv, device):
        return pltpu.make_async_remote_copy(
            source, target, send, recv, device_id=device, device_id_type=MESH
        )

    def is_later(dy, dk):
        return (k ^ dk) * 2 + (ylo ^ dy) > k * 2 + ylo

    sibling = (chip * 2 + 1 - core, pair)
    beside = [((chip ^ 1) * 2 + core, pair), ((chip ^ 1) * 2 + 1 - core, pair)]
    pair_peers = [pair ^ n for n in (5, 7, 4, 6, 3, 1, 2)]
    y = yhi * 2 + ylo

    def at(x, y, z):
        return (((y % 2) * 8 + z) * 2 + core, x * 2 + y // 2)

    hops = (
        (at((x + 1) % 4, y, z), x < 3),
        (at((x + 3) % 4, y, z), x > 0),
        (at(x, (y + 1) % 4, z), y < 3),
        (at(x, (y + 3) % 4, z), y > 0),
        (at(x, y, (z + 1) % 8), k < 3),
        (at(x, y, (z + 7) % 8), k > 0),
        (sibling, None),
    )

    def for_hops(condition, act):
        for n, (device, there) in enumerate(hops):
            @pl.when(condition if there is None else jnp.logical_and(condition, there))
            def _():
                act(n, device)

    kg_load = pltpu.make_async_copy(kg_hbm, kgin, load_sem.at[0])
    kg_load.start()

    barrier = pltpu.get_barrier_semaphore()

    def is_later_pair(other):
        return (other % 2) * 4 + other // 2 > yhi * 4 + x

    @pl.when(early)
    def _():
        for dy, dk in DIRECT:
            signal(barrier, peer(1, dy, dk))
        for dy, dk in OWN:
            @pl.when(is_later(dy, dk))
            def _():
                signal(barrier, peer(0, dy, dk))
        for other in pair_peers:
            @pl.when(is_later_pair(other))
            def _():
                signal(barrier, (row, other))
        signal(barrier, sibling)
        @pl.when(k % 2 == 0)
        def _():
            signal(barrier, beside[1])

    for_hops(late, lambda n, device: signal(barrier, device))

    sa_load = pltpu.make_async_copy(sa_hbm, sa, load_sem.at[1])
    sa_load.start()
    d2_load = pltpu.make_async_copy(d2_hbm, d2, load_sem.at[2])
    d2_load.start()
    d1_load = pltpu.make_async_copy(d1_hbm, d1, load_sem.at[3])
    d1_load.start()
    kw_load = pltpu.make_async_copy(kw_hbm, kw, load_sem.at[4])
    kw_load.start()
    g_loads = []
    for p in range(2):
        for h in range(2):
            load = pltpu.make_async_copy(
                g_hbm.at[p, :, pl.ds(h * 24, 24), :], gbuf.at[p, h], load_sem.at[5 + 2 * p + h]
            )
            g_loads.append(load)

    kg_load.wait()
    kg[0, core, 0] = jnp.concatenate([kgin[0:24, :], kgin[24:48, :]], axis=1)

    def inner(v):
        return jnp.where(jnp.logical_or(v == 0, v == 3), 0, 1)

    pl.semaphore_wait(
        barrier, jnp.where(early, 1 + 2 * k + ylo + 4 * yhi + x + k % 2, 8 + inner(x) + inner(y) + inner(k))
    )

    own = {}
    for n, (dy, dk) in enumerate(OWN):
        own[dy, dk] = remote(
            kg.at[0, core, 0], kg.at[0, core, own_slot(dy, dk)], own_send.at[n], own_recv.at[n], peer(0, dy, dk)
        )
    cut = {}
    for n, (dy, dk) in enumerate(DIRECT):
        cut[dy, dk] = remote(
            kg.at[0, core, 0], kg.at[1, core, cut_slot(dy, dk)], cut_send.at[n], cut_recv.at[n], peer(1, dy, dk)
        )

    @pl.when(late)
    def _():
        for copy in cut.values():
            copy.start()
        for n, (dy, dk) in enumerate(DIRECT):
            signal(far_here.at[n], peer(1, dy, dk))
        for_hops(late, lambda n, device: signal(hop_here.at[0, n ^ 1 if n < 6 else n], device))

    @pl.when(early)
    def _():
        for n, (dy, dk) in enumerate(OWN):
            @pl.when(jnp.logical_not(is_later(dy, dk)))
            def _():
                signal(near_here.at[n], peer(0, dy, dk))
                own[dy, dk].start()
        for n, other in enumerate(pair_peers):
            @pl.when(jnp.logical_not(is_later_pair(other)))
            def _():
                signal(pair_here.at[n], (row, other))
        @pl.when(k % 2 == 1)
        def _():
            signal(pair_here.at[7], beside[1])

    def next_round(step):
        for_hops(late, lambda n, device: pl.semaphore_wait(hop_here.at[step, n], 1))
        if step < 3:
            for_hops(late, lambda n, device: signal(hop_here.at[step + 1, n ^ 1 if n < 6 else n], device))

    sa_load.wait()
    high, low = split(sa[...].reshape(128, 512))
    w[0:128] = high
    w[128:256] = low
    d2_load.wait()
    for load in g_loads:
        load.start()
    cross(d2, w, s8, range(4))
    next_round(0)
    cross(d2, w, s8, range(4, 8))
    fall[0, core, 0] = as_row(s8)
    next_round(1)
    f_own = {}
    for n, (dy, dk) in enumerate(OWN):
        f_own[dy, dk] = remote(
            fall.at[0, core, 0], fall.at[0, core, own_slot(dy, dk)], f_send.at[n], f_recv.at[n], peer(0, dy, dk)
        )
    f_cut = {}
    for n, (dy, dk) in enumerate(DIRECT):
        f_cut[dy, dk] = remote(
            fall.at[0, core, 0], fall.at[1, core, cut_slot(dy, dk)], f_send.at[7 + n], f_recv.at[7 + n], peer(1, dy, dk)
        )

    @pl.when(late)
    def _():
        for copy in f_cut.values():
            copy.start()
        next_round(2)
        for dy, dk in OWN:
            own[dy, dk].start()
        for copy in f_own.values():
            copy.start()

    @pl.when(early)
    def _():
        for n, (dy, dk) in enumerate(OWN):
            @pl.when(is_later(dy, dk))
            def _():
                pl.semaphore_wait(near_here.at[n], 1)
                own[dy, dk].start()
        for copy in f_own.values():
            copy.start()

    for load in g_loads:
        load.wait()

    def split_general(n, _):
        p, h, c = n // 4, (n // 2) % 2, n % 2

        def put(high, low, chips):
            for s in range(0, len(chips), 2):
                a, b = split(jnp.concatenate([gbuf[p, h, chips[s + i] * 2 + c] for i in range(2)], axis=0))
                high[s * 24:s * 24 + 48, :] = a
                low[s * 24:s * 24 + 48, :] = b

        put(ghi.at[p, h, c], glo.at[p, h, c], [chip_of(0, s // 4, s % 4) for s in range(8)])
        for part in range(2):
            chips = [chip_of(1, s % 2, ORDER[s // 2]) for s in range(4 * part, 4 * part + 4)]
            put(cut_hi.at[part, p, h, c], cut_lo.at[part, p, h, c], chips)
        return 0

    lax.fori_loop(0, 8, split_general, 0)

    @pl.when(early)
    def _():
        for n, (dy, dk) in enumerate(DIRECT):
            pl.semaphore_wait(far_here.at[n], 1)
            cut[dy, dk].start()
        for copy in f_cut.values():
            copy.start()

    @pl.when(jnp.logical_and(early, k % 2 == 0))
    def _():
        pl.semaphore_wait(pair_here.at[7], 1)


    def handed_on(array, send, recv):
        copies = {}
        for n, dk in enumerate((3, 1)):
            mine = array.at[1, core, pl.ds(cut_slot(0, dk), 2)]
            theirs = array.at[1, core, pl.ds(cut_slot(0, dk ^ 1), 2)]
            for m, (target, device) in enumerate(((theirs, beside[0]), (theirs, beside[1]), (mine, sibling))):
                copies[n, m] = remote(mine, target, send.at[n, m], recv.at[n, m], device)
        return copies

    def hand_on(arriving, copies):
        for n, dk in enumerate((3, 1)):
            for dy in range(2):
                arriving[dy, dk].wait_recv()
            for m in range(3):
                copies[n, m].start()

    passes = handed_on(kg, pass_send, pass_recv)
    f_passes = handed_on(fall, f_pass_send, f_pass_recv)

    def rotate(blocks, high_of, low_of):
        rows = blocks.reshape(-1, 128)
        depth = 2 * rows.shape[0]
        x = rows.T
        high, low = split(jnp.concatenate([x[0:64], x[64:128]], axis=1))
        both = jnp.concatenate([high, low], axis=0)
        result = []
        for p in range(2):
            a = lax.dot_general(both, high_of(p).reshape(depth, 512), PLAIN, preferred_element_type=F32)
            b = lax.dot_general(high, low_of(p).reshape(depth, 512), PLAIN, preferred_element_type=F32)
            result.append(a[0:64] + a[64:128] + b)
        return result

    def rotate_cut(part):
        return rotate(kg[1, :, 4 * part:4 * part + 4], lambda p: cut_hi[part, p], lambda p: cut_lo[part, p])

    hand_on(cut, passes)
    for copy in own.values():
        copy.wait_recv()
    over = remote(kg.at[0, core], kg.at[0, core], sib_send.at[0], sib_recv.at[0], sibling)
    over.start()
    over.wait_recv()
    for p, part in enumerate(rotate(kg[0], lambda p: ghi[p], lambda p: glo[p])):
        moved[p] = part

    for copy in f_own.values():
        copy.wait_recv()
    f_over = remote(fall.at[0, core], fall.at[0, core], sib_send.at[1], sib_recv.at[1], sibling)
    f_over.start()
    hand_on(f_cut, f_passes)
    for n in range(2):
        passes[n, 2].wait_recv()
    for p, part in enumerate(rotate_cut(0)):
        moved[p] = moved[p] + part
    lane = lax.broadcasted_iota(jnp.int32, (1, 128), 1)

    def turn(part, acc):
        acc = list(acc)
        for slot in range(8):
            first = 4 * (chip_of(1, slot % 2, ORDER[slot // 2]) if part else chip_of(0, slot // 4, slot % 4))
            for c in range(2):
                f = fall[part, c, slot]
                q = first + 2 * c
                for p in range(2):
                    acc[p] = acc[p] + f * jnp.where(lane < 64, kw[p, q], kw[p, q + 1])
        return acc

    kw_load.wait()
    f_over.wait_recv()
    acc = turn(0, [jnp.zeros((1, 128), F32) for _ in range(2)])
    d1_load.wait()
    high, low = split(jnp.broadcast_to(d1[...], (16, 512)))
    line = lax.broadcasted_iota(jnp.int32, (16, 512), 0)
    ones = jnp.where(line == 0, high.astype(F32), jnp.where(line == 1, low.astype(F32), 0.0)).astype(BF16)
    for n in range(2):
        for m in range(2):
            passes[n, m].wait_recv()
    for p, part in enumerate(rotate_cut(1)):
        high, low = split(moved[p] + part)
        w[64 * p:64 * p + 64] = high
        w[128 + 64 * p:192 + 64 * p] = low
    cross(d2, w, s8)
    exchange = as_row(s8)
    c = lax.dot_general(ones, w[...], ROW_BY_ROW, preferred_element_type=F32)
    c = c[0:1] + c[1:2]
    coulomb = c[:, 0:128] + c[:, 128:256]

    for copy in f_passes.values():
        copy.wait_recv()
    acc = turn(1, acc)
    turned = jnp.concatenate([a[:, 0:64] + a[:, 64:128] for a in acc], axis=1)

    next_round(3)
    pbuf[pair] = exchange + 2.0 * coulomb + turned
    p_copies = []
    for n, other in enumerate(pair_peers):
        @pl.when(jnp.logical_and(early, is_later_pair(other)))
        def _():
            pl.semaphore_wait(pair_here.at[n], 1)

        copy = remote(pbuf.at[pair], pbuf.at[pair], p_send.at[n], p_recv.at[n], (row, other))
        copy.start()
        p_copies.append(copy)
    for copies in (own.values(), cut.values(), passes.values(), f_own.values(), f_cut.values(), f_passes.values(), (over, f_over)):
        for copy in copies:
            copy.wait_send()
    for copy in p_copies:
        copy.wait_recv()
    total = pbuf[0]
    for n in range(1, 8):
        total = total + pbuf[n]
    total = 2.0 * total
    out_ref[0:1, :] = total[:, 0:64]
    out_ref[1:2, :] = total[:, 64:128]
    for copy in p_copies:
        copy.wait_send()


def per_device(slab_active, slab_general, kappa_general, kappa_window, density_one, density_two):
    dma, regular = pltpu.SemaphoreType.DMA, pltpu.SemaphoreType.REGULAR
    return pl.pallas_call(
        kernel,
        out_shape=jax.ShapeDtypeStruct((2, 64), F32),
        in_specs=[pl.BlockSpec(memory_space=pltpu.HBM)] * 6,
        out_specs=pl.BlockSpec(memory_space=pltpu.VMEM),
        scratch_shapes=[
            pltpu.VMEM((2, 64, 512), F32),
            pltpu.VMEM((2, 2, 32, 24, 512), F32),
            pltpu.VMEM((48, 64), F32),
            pltpu.SMEM((2, 64), F32),
            pltpu.VMEM((1, 512), F32),
            pltpu.VMEM((64, 64, 512), BF16),
            pltpu.VMEM((2, 2, 2, 192, 512), BF16),
            pltpu.VMEM((2, 2, 2, 192, 512), BF16),
            pltpu.VMEM((2, 2, 2, 2, 96, 512), BF16),
            pltpu.VMEM((2, 2, 2, 2, 96, 512), BF16),
            pltpu.VMEM((2, 2, 8, 24, 128), F32),
            pltpu.VMEM((256, 512), BF16),
            pltpu.VMEM((64, 8, 256), F32),
            pltpu.VMEM((2, 64, 512), F32),
            pltpu.VMEM((2, 2, 8, 1, 128), F32),
            pltpu.VMEM((8, 1, 128), F32),
            dma((9,)),
            regular((7,)),
            regular((4,)),
            regular((8,)),
            regular((4, 7)),
            dma((7,)),
            dma((7,)),
            dma((4,)),
            dma((4,)),
            dma((2, 3)),
            dma((2, 3)),
            dma((2,)),
            dma((2,)),
            dma((11,)),
            dma((11,)),
            dma((2, 3)),
            dma((2, 3)),
            dma((7,)),
            dma((7,)),
        ],
        compiler_params=pltpu.CompilerParams(
            collective_id=0, has_side_effects=True, vmem_limit_bytes=48 * 2**20
        ),
        name="sigma",
    )(*(
        pltpu.with_memory_space_constraint(x, pltpu.HBM)
        for x in (
            slab_active,
            slab_general.reshape(2, 32, 48, 512),
            kappa_general,
            kappa_window,
            density_one.reshape(1, 512),
            density_two,
        )
    ))


def solution(mesh):
    in_specs = (
        P("rows", None, "pairs"),
        P("rows", None, "pairs"),
        P("rows", None),
        P("rows", None),
        P("pairs"),
        P(None, None, "pairs"),
    )
    out_specs = P("rows", None)
    return jax.shard_map(
        per_device, mesh=mesh, in_specs=in_specs, out_specs=out_specs, check_vma=False
    )
```
